32 devices in a mesh: groups: 2 (over y), tensor: 2 (over x), expert: 4 (over z), dp: 2 (over core).
Axes of the slice: x: 2, y: 2, z: 4, core: 2. Of those that a mesh axis runs over, the one named last changes fastest.
Arguments:
- tokens: bfloat16 [32, 6144], P(('groups', 'tensor', 'expert', 'dp')), parts along dimension 0, may hold values from -6 to 6
- routes: int32 [32, 2], P(('groups', 'tensor', 'expert', 'dp')), parts along dimension 0, may hold values from 0 to 3, all different within a row; in each aligned block of 1 rows (0 to 0, 1 to 1, ...) no two rows name the same one
- gates: float32 [32, 2], P(('groups', 'tensor', 'expert', 'dp')), parts along dimension 0, may hold values from 0.1 to 0.9
- w_gate: bfloat16 [4, 6144, 8192], P('expert', 'dp', 'tensor'), may hold values from -0.078125 to 0.078125
- w_up: bfloat16 [4, 6144, 8192], P('expert', 'dp', 'tensor'), may hold values from -0.078125 to 0.078125
- w_down: bfloat16 [4, 8192, 6144], P('expert', 'tensor', 'dp'), may hold values from -0.0625 to 0.0625
Outputs:
- mixed: bfloat16 [32, 6144], P(('groups', 'tensor', 'expert', 'dp')), parts along dimension 0
The draws below stay inside these ranges and needn't reach their ends.
There are 2 independent parts, one for each index of `groups`. The reference program is written for one: setup_inputs(seed, part) draws one part's arguments, and reference() takes and returns one part's arrays. A program takes and returns all parts, laid end to end along the dimension named above; an argument that names none is the same for every part. Nothing has to cross between parts.
Inputs may be any that keep to these rules, and one draw needn't show every extreme that they name: `routes`: each row names two different experts, and every expert is named by some row.
All inputs are finite; a program needn't handle non-finite values.
Results may differ from the reference program's by a relative error of at most 0.009.
Values may be sent and summed in bfloat16 or wider, within the bound.
A program may use at most 448 MiB of HBM per device.

```python
import math
import jax
import jax.numpy as jnp
import numpy as np
from jax import lax

D = 6144
FF = 8192
TOK_DEV = 1
EXPERTS = 4
TOKENS = 16
N_TENSOR = 2


def shard_levels(rng, shape, pieces, smallest, high):
    level, own = 1.0, jax.random.fold_in(rng, 6)
    for position, parts in pieces:
        heights = jnp.exp(jax.random.uniform(jax.random.fold_in(own, position), (parts,), jnp.float32, smallest / len(pieces), high / len(pieces)))
        level = level * jnp.repeat(heights, shape[position] // parts).reshape([-1 if axis == position else 1 for axis in range(len(shape))])
    return level


def routed_block(own_key, own, number, rows, count, top, limit, slope):
    sequence = jax.random.permutation(own_key, count)
    packed, ordinary = load_shares(count, rows * top, limit, slope, True), load_shares(count, rows * top, limit, slope, False)
    places = jnp.arange(count)

    def named(sizes, turn):
        used = int((sizes > 0).sum())
        fixed = max(1, used // 4)
        moved = fixed + (places - fixed + turn * (used - fixed)) % max(1, count - fixed)
        return jnp.zeros((count,), jnp.int32).at[sequence[jnp.where(places < fixed, places, moved)]].set(jnp.asarray(sizes, jnp.int32))

    sizes = jnp.where(number % 4 == 0, named(packed, number // 4), named(ordinary, number - number // 4 - 1))
    mixed = jax.random.permutation(jax.random.fold_in(own, 3), count)
    source_of, sink = mixed[0:count // 2 * 2:2], mixed[1:count // 2 * 2:2]
    room = jnp.minimum(sizes[source_of] - 1, limit - sizes[sink]) // 2
    room = jnp.where((source_of == sequence[0]) | (sink == sequence[0]) | (sizes[sink] == 0), 0, jnp.maximum(room, 0))
    moved = jax.random.randint(jax.random.fold_in(own, 4), (count // 2,), 0, 1 << 20) % (room + 1)
    sizes = sizes.at[source_of].add(-moved).at[sink].add(moved)
    members = jnp.searchsorted(jnp.cumsum(sizes), jnp.arange(rows * top), side="right").astype(jnp.int32)
    listing = members.reshape(top, rows).T
    listing = listing[jax.random.permutation(jax.random.fold_in(own, 1), rows)]
    turn = jax.random.randint(jax.random.fold_in(own, 2), (rows, 1), 0, top)
    return jnp.take_along_axis(listing, (jnp.arange(top)[None, :] + turn) % top, axis=1)


def load_shares(number_of, total, bound, slope, full):
    weights = [(1 << 20) // math.isqrt(rank ** slope) + 1 for rank in range(1, number_of + 1)]
    largest = bound if full else min(bound, max(-(-total // number_of), total * weights[0] // sum(weights)))
    least = 1 if total - largest >= number_of - 1 else 0
    holding, rest = [largest] + [least] * (number_of - 1), total - largest - least * (number_of - 1)
    while rest > 0:
        movable = [i for i in range(1, number_of) if holding[i] < largest] or [i for i in range(1, number_of) if holding[i] < bound]
        mass, left = sum([weights[i] for i in movable]), rest
        for i in movable:
            addition = min(bound - holding[i], max(1, left * weights[i] // mass), rest)
            holding[i] = holding[i] + addition
            rest = rest - addition
    return np.array(holding)


def gaussian(stream_key, extent, width, limit, pieces=(), held_as=jnp.bfloat16):
    level = shard_levels(stream_key, extent, pieces, -0.22, 0.18) if pieces else 1.0
    drawn = jax.random.normal(stream_key, extent, jnp.float32) * width * level
    return jnp.minimum(jnp.maximum(drawn, -limit), limit).astype(held_as)


def setup_inputs(seed: int = 0, part: int = 0) -> dict:
    key_of = jax.random.split(jax.random.key(seed), 7)
    own_keys = jax.random.split(jax.random.fold_in(key_of[6], part), 7)
    tokens = gaussian(own_keys[0], (TOKENS, D), 1.0, 6.0, ((0, 16),))
    routes_keys = jax.random.split(jax.random.fold_in(own_keys[1], 1), TOKENS // TOK_DEV)
    routes_turns = jax.random.permutation(jax.random.fold_in(own_keys[1], 3), TOKENS // TOK_DEV)
    routes = jax.vmap(lambda own, number: routed_block(jax.random.fold_in(own_keys[1], 2), own, number, TOK_DEV, EXPERTS, 2, TOK_DEV, 2))(routes_keys, routes_turns).reshape((TOKENS, 2))
    gates = jnp.clip(0.1 + 0.79999997 * jax.random.uniform(own_keys[2], (TOKENS, 2), jnp.float32) ** shard_levels(own_keys[2], (TOKENS, 2), ((0, 16),), -0.2, 0.2), 0.1, 0.9)
    w_gate = gaussian(key_of[3], (EXPERTS, D, FF), D ** -0.5, 0.078125, ((0, 4), (1, 2), (2, 2)))
    w_up = gaussian(key_of[4], (EXPERTS, D, FF), D ** -0.5, 0.078125, ((0, 4), (1, 2), (2, 2)))
    w_down = gaussian(key_of[5], (EXPERTS, FF, D), FF ** -0.5, 0.0625, ((0, 4), (1, 2), (2, 2)))
    return {"tokens": tokens, "routes": routes, "gates": gates, "w_gate": w_gate, "w_up": w_up, "w_down": w_down}


def reference(tokens, routes, gates, w_gate, w_up, w_down):
    slice_width = FF // N_TENSOR
    mixed = jnp.zeros((TOKENS, D), jnp.float32)
    for expert_id in range(EXPERTS):
        weight = jnp.sum(gates * (routes == expert_id).astype(jnp.float32), axis=1)
        gate_val = jnp.dot(tokens, w_gate[expert_id], preferred_element_type=jnp.float32)
        up_val = jnp.dot(tokens, w_up[expert_id], preferred_element_type=jnp.float32)
        hidden = (jax.nn.silu(gate_val) * up_val).astype(jnp.bfloat16)
        hidden_slices = hidden.reshape(TOKENS, N_TENSOR, slice_width).transpose(1, 0, 2)
        down_slices = w_down[expert_id].reshape(N_TENSOR, slice_width, D)

        def add_slice(total, pair):
            part = jnp.dot(pair[0], pair[1], preferred_element_type=jnp.float32).astype(jnp.bfloat16)
            part = lax.optimization_barrier(part)
            return total + part.astype(jnp.float32), None

        summed, _ = lax.scan(add_slice, jnp.zeros((TOKENS, D), jnp.float32), (hidden_slices, down_slices))
        expert_out = summed.astype(jnp.bfloat16)
        mixed = mixed + weight[:, None] * expert_out.astype(jnp.float32)
    return mixed.astype(jnp.bfloat16)
```

```python
import functools

import jax
import jax.numpy as jnp
from jax import lax
from jax.experimental import pallas as pl
from jax.experimental.pallas import tpu as pltpu
from jax.sharding import PartitionSpec as P

AXES = ("groups", "tensor", "expert", "dp")
SUB = 8


def remote(src, dst, send_sem, recv_sem, where):
    return pltpu.make_async_remote_copy(
        src_ref=src,
        dst_ref=dst,
        send_sem=send_sem,
        recv_sem=recv_sem,
        device_id=where,
        device_id_type=pl.DeviceIdType.MESH,
    )


def kernel(
    sizes, tok_ref, routes_ref, gates_ref, wg_hbm, wu_hbm, wd_hbm, out_ref,
    wg, wu, wd, tstage, tsend, tline, tall, tflat, x, pown, psend, precv, hid,
    osend, orecv, zstage, zsend, zrecv,
    w_sem, ts_send, ts_recv, tq_send, tq_recv, p_send, p_recv, o_send, o_recv, z_send, z_recv,
):
    n_groups, n_tensor, n_expert, n_dp = sizes
    n_quad, n_line = n_groups * n_tensor, n_expert * n_dp
    nf, _, cf = wg.shape
    nd, ffh, cd = wd.shape
    lanes = tstage.shape[1]
    g, t = lax.axis_index("groups"), lax.axis_index("tensor")
    e, d = lax.axis_index("expert"), lax.axis_index("dp")
    quad, line = g * n_tensor + t, e * n_dp + d

    def line_peer(k):
        peer = lax.rem(line + k, n_line)
        return peer, {"groups": g, "tensor": t, "expert": peer // n_dp, "dp": lax.rem(peer, n_dp)}

    def quad_peer(k):
        peer = lax.rem(quad + k, n_quad)
        return peer, {"groups": peer // n_tensor, "tensor": lax.rem(peer, n_tensor), "expert": e, "dp": d}

    sibling = {"groups": g, "tensor": t, "expert": e, "dp": 1 - d}

    loads = []
    for j in range(nf):
        cols = pl.ds(pl.multiple_of(g * ffh + j * cf, 128), cf)
        loads.append(pltpu.make_async_copy(wg_hbm.at[0, :, cols], wg.at[j], w_sem.at[0, j]))
        loads.append(pltpu.make_async_copy(wu_hbm.at[0, :, cols], wu.at[j], w_sem.at[1, j]))
    half = pl.ds(pl.multiple_of(g * ffh, 16), ffh)
    for j in range(nd):
        loads.append(pltpu.make_async_copy(wd_hbm.at[0, half, pl.ds(j * cd, cd)], wd.at[j], w_sem.at[2, j]))
    for load in loads:
        load.start()

    barrier = pltpu.get_barrier_semaphore()
    for k in range(1, n_line):
        pl.semaphore_signal(barrier, inc=1, device_id=line_peer(k)[1], device_id_type=pl.DeviceIdType.MESH)
    for k in range(1, n_quad):
        pl.semaphore_signal(barrier, inc=1, device_id=quad_peer(k)[1], device_id_type=pl.DeviceIdType.MESH)

    for k in range(n_dp * SUB):
        tstage[k : k + 1, :] = tok_ref[0:1, k * lanes : (k + 1) * lanes].astype(jnp.float32)
    for h in range(n_dp):
        tsend[h] = tstage[h * SUB : (h + 1) * SUB, :].astype(jnp.bfloat16)
    pl.semaphore_wait(barrier, n_line - 1 + n_quad - 1)

    sends = []
    for k in range(1, n_line):
        peer, where = line_peer(k)
        copy = remote(tsend.at[lax.rem(peer, n_dp)], tline.at[line], ts_send.at[k], ts_recv.at[k], where)
        copy.start()
        sends.append(copy)
    tline[line] = tsend[d]
    for k in range(1, n_line):
        source = lax.rem(line + n_line - k, n_line)
        remote(tsend.at[0], tline.at[source], ts_send.at[k], ts_recv.at[k], sibling).wait_recv()

    for k in range(1, n_quad):
        copy = remote(tline, tall.at[quad], tq_send.at[k], tq_recv.at[k], quad_peer(k)[1])
        copy.start()
        sends.append(copy)
    tall[quad] = tline[...]
    for k in range(1, n_quad):
        source = lax.rem(quad + n_quad - k, n_quad)
        remote(tline, tall.at[source], tq_send.at[k], tq_recv.at[k], sibling).wait_recv()
    pair = 2 * n_line
    for p in range(n_quad // 2):
        for i in range(2):
            for s in range(n_line):
                row = (i * n_line + s) * SUB
                block = tall[2 * p + i, s].astype(jnp.float32)
                for b in range(lanes // 128):
                    tflat[b, row : row + SUB, :] = block[:, b * 128 : (b + 1) * 128]
        for s in range(SUB):
            for b in range(lanes // 128):
                part = tflat[b, pl.ds(s, pair, stride=SUB), :]
                col = s * lanes + b * 128
                x[p * pair : (p + 1) * pair, col : col + 128] = part.astype(jnp.bfloat16)

    def finish(j):
        remote(psend.at[j], precv.at[j], p_send.at[j], p_recv.at[j], sibling).wait_recv()
        gate = pown[j, 0] + precv[j, 0].astype(jnp.float32)
        up = pown[j, 1] + precv[j, 1].astype(jnp.float32)
        hid[:, j * cf : (j + 1) * cf] = (gate / (1.0 + jnp.exp(-gate)) * up).astype(jnp.bfloat16)

    for j in range(nf):
        for i, w in enumerate((wg, wu)):
            loads[2 * j + i].wait()
            part = jnp.dot(x[...], w[j], preferred_element_type=jnp.float32)
            pown[j, i] = part
            psend[j, i] = part.astype(jnp.bfloat16)
        copy = remote(psend.at[j], precv.at[j], p_send.at[j], p_recv.at[j], sibling)
        copy.start()
        sends.append(copy)
        if j > 0:
            finish(j - 1)
    finish(nf - 1)

    for j in range(nd):
        loads[2 * nf + j].wait()
        part = jnp.dot(hid[...], wd[j], preferred_element_type=jnp.float32)
        for q in range(n_quad):
            block = part[q * n_line : (q + 1) * n_line]
            osend[j, q] = jnp.concatenate([block[:, :lanes], block[:, lanes:]], axis=0).astype(jnp.bfloat16)
        for k in range(1, n_quad):
            peer, where = quad_peer(k)
            copy = remote(osend.at[j, peer], orecv.at[j, quad], o_send.at[j, k], o_recv.at[j, k], where)
            copy.start()
            sends.append(copy)

    for j in range(nd):
        total = osend[j, quad].astype(jnp.float32)
        for k in range(1, n_quad):
            source = lax.rem(quad + n_quad - k, n_quad)
            remote(osend.at[j, 0], orecv.at[j, source], o_send.at[j, k], o_recv.at[j, k], sibling).wait_recv()
            total += orecv[j, source].astype(jnp.float32)
        for i in range(2):
            for b in range(lanes // 128):
                part = total[i * n_line : (i + 1) * n_line, b * 128 : (b + 1) * 128]
                zstage[b, pl.ds(2 * j + i, n_line, stride=SUB), :] = part
    for s in range(n_line):
        for b in range(lanes // 128):
            part = zstage[b, s * SUB : (s + 1) * SUB, :]
            zsend[s, :, b * 128 : (b + 1) * 128] = part.astype(jnp.bfloat16)
    for k in range(1, n_line):
        peer, where = line_peer(k)
        copy = remote(zsend.at[peer], zrecv.at[line], z_send.at[k], z_recv.at[k], where)
        copy.start()
        sends.append(copy)
    zrecv[line] = zsend[line]
    for k in range(1, n_line):
        source = lax.rem(line + n_line - k, n_line)
        remote(zsend.at[0], zrecv.at[source], z_send.at[k], z_recv.at[k], sibling).wait_recv()

    for h in range(n_dp):
        total = jnp.zeros((SUB, lanes), jnp.float32)
        for i in range(n_expert):
            weight = jnp.float32(0)
            for c in range(routes_ref.shape[1]):
                weight += jnp.where(routes_ref[0, c] == i, gates_ref[0, c], jnp.float32(0))
            total += weight * zrecv[i * n_dp + h].astype(jnp.float32)
        tstage[h * SUB : (h + 1) * SUB, :] = total
    for k in range(n_dp * SUB):
        out_ref[0:1, k * lanes : (k + 1) * lanes] = tstage[k : k + 1, :].astype(jnp.bfloat16)
    for copy in sends:
        copy.wait_send()


def shards(sizes, tokens, routes, gates, w_gate, w_up, w_down):
    n_groups, n_tensor, n_expert, n_dp = sizes
    n_quad, n_line = n_groups * n_tensor, n_expert * n_dp
    rows = n_quad * n_line
    depth, ffh = w_gate.shape[1], w_gate.shape[2] // n_groups
    cf = min(256, ffh)
    nf = ffh // cf
    lanes = depth // SUB
    cd = 2 * lanes
    nd = depth // cd
    bf16, f32 = jnp.bfloat16, jnp.float32
    dma = pltpu.SemaphoreType.DMA
    return pl.pallas_call(
        functools.partial(kernel, sizes),
        out_shape=jax.ShapeDtypeStruct(tokens.shape, bf16),
        in_specs=[
            pl.BlockSpec(memory_space=pltpu.VMEM),
            pl.BlockSpec(memory_space=pltpu.SMEM),
            pl.BlockSpec(memory_space=pltpu.SMEM),
            pl.BlockSpec(memory_space=pl.ANY),
            pl.BlockSpec(memory_space=pl.ANY),
            pl.BlockSpec(memory_space=pl.ANY),
        ],
        out_specs=pl.BlockSpec(memory_space=pltpu.VMEM),
        scratch_shapes=[
            pltpu.VMEM((nf, depth, cf), bf16),
            pltpu.VMEM((nf, depth, cf), bf16),
            pltpu.VMEM((nd, ffh, cd), bf16),
            pltpu.VMEM((n_dp * SUB, lanes), f32),
            pltpu.VMEM((n_dp, SUB, lanes), bf16),
            pltpu.VMEM((n_line, SUB, lanes), bf16),
            pltpu.VMEM((n_quad, n_line, SUB, lanes), bf16),
            pltpu.VMEM((lanes // 128, 2 * n_line * SUB, 128), f32),
            pltpu.VMEM((rows, depth), bf16),
            pltpu.VMEM((nf, 2, rows, cf), f32),
            pltpu.VMEM((nf, 2, rows, cf), bf16),
            pltpu.VMEM((nf, 2, rows, cf), bf16),
            pltpu.VMEM((rows, ffh), bf16),
            pltpu.VMEM((nd, n_quad, 2 * n_line, lanes), bf16),
            pltpu.VMEM((nd, n_quad, 2 * n_line, lanes), bf16),
            pltpu.VMEM((lanes // 128, n_line * SUB, 128), f32),
            pltpu.VMEM((n_line, SUB, lanes), bf16),
            pltpu.VMEM((n_line, SUB, lanes), bf16),
            dma((3, max(nf, nd))),
            dma((n_line,)),
            dma((n_line,)),
            dma((n_quad,)),
            dma((n_quad,)),
            dma((nf,)),
            dma((nf,)),
            dma((nd, n_quad)),
            dma((nd, n_quad)),
            dma((n_line,)),
            dma((n_line,)),
        ],
        compiler_params=pltpu.CompilerParams(
            collective_id=0, has_side_effects=True, vmem_limit_bytes=56 * 1024 * 1024
        ),
    )(tokens, routes, gates, w_gate, w_up, w_down)


def solution(mesh):
    placed = (
        P(AXES, None),
        P(AXES, None),
        P(AXES, None),
        P("expert", "dp", "tensor"),
        P("expert", "dp", "tensor"),
        P("expert", "tensor", "dp"),
    )
    return jax.shard_map(
        functools.partial(shards, tuple(mesh.shape[axis] for axis in AXES)),
        mesh=mesh,
        in_specs=placed,
        out_specs=P(AXES, None),
        check_vma=False,
    )
```

```python
import functools

import jax
import jax.numpy as jnp
from jax import lax
from jax.experimental import pallas as pl
from jax.experimental.pallas import tpu as pltpu
from jax.sharding import PartitionSpec as P

AXES = ("groups", "tensor", "expert", "dp")
SUB = 8


def remote(src, dst, send_sem, recv_sem, where):
    return pltpu.make_async_remote_copy(
        src_ref=src,
        dst_ref=dst,
        send_sem=send_sem,
        recv_sem=recv_sem,
        device_id=where,
        device_id_type=pl.DeviceIdType.MESH,
    )


def kernel(
    sizes, tok_ref, routes_ref, gates_ref, wg_hbm, wu_hbm, wd_hbm, out_ref,
    wg, wu, wd, tstage, tsend, tline, tall, tflat, x, pown, psend, precv, hid,
    osend, orecv, zstage, zsend, zrecv,
    w_sem, ts_send, ts_recv, tq_send, tq_recv, p_send, p_recv, o_send, o_recv, z_send, z_recv,
):
    n_groups, n_tensor, n_expert, n_dp = sizes
    n_quad, n_line = n_groups * n_tensor, n_expert * n_dp
    nf, _, cf = wg.shape
    nd, ffh, cd = wd.shape
    lanes = tstage.shape[1]
    pieces = cd // lanes
    g, t = lax.axis_index("groups"), lax.axis_index("tensor")
    e, d = lax.axis_index("expert"), lax.axis_index("dp")
    quad, line = g * n_tensor + t, e * n_dp + d

    def ahead(at, n):
        return [at] + [jnp.where(at + k >= n, at + k - n, at + k) for k in range(1, n)]

    def behind(at, n):
        return [at] + [jnp.where(at >= k, at - k, at + n - k) for k in range(1, n)]

    to_g, to_t, to_e, to_d = ahead(g, n_groups), ahead(t, n_tensor), ahead(e, n_expert), ahead(d, n_dp)
    from_g, from_t, from_e, from_d = behind(g, n_groups), behind(t, n_tensor), behind(e, n_expert), behind(d, n_dp)

    def line_peer(k):
        pe, pd = to_e[k // n_dp], to_d[k % n_dp]
        return pe * n_dp + pd, {"groups": g, "tensor": t, "expert": pe, "dp": pd}

    def line_source(k):
        return from_e[k // n_dp] * n_dp + from_d[k % n_dp]

    def quad_peer(k):
        pg, pt = to_g[k // n_tensor], to_t[k % n_tensor]
        return pg * n_tensor + pt, {"groups": pg, "tensor": pt, "expert": e, "dp": d}

    def quad_source(k):
        return from_g[k // n_tensor] * n_tensor + from_t[k % n_tensor]

    sibling = {"groups": g, "tensor": t, "expert": e, "dp": 1 - d}

    loads = []
    for j in range(nf):
        cols = pl.ds(pl.multiple_of(g * ffh + j * cf, 128), cf)
        loads.append(pltpu.make_async_copy(wg_hbm.at[0, :, cols], wg.at[j], w_sem.at[0, j]))
        loads.append(pltpu.make_async_copy(wu_hbm.at[0, :, cols], wu.at[j], w_sem.at[1, j]))
    half = pl.ds(pl.multiple_of(g * ffh, 16), ffh)
    for j in range(nd):
        loads.append(pltpu.make_async_copy(wd_hbm.at[0, half, pl.ds(j * cd, cd)], wd.at[j], w_sem.at[2, j]))
    for load in loads:
        load.start()

    barrier = pltpu.get_barrier_semaphore()
    for k in range(1, n_line):
        pl.semaphore_signal(barrier, inc=1, device_id=line_peer(k)[1], device_id_type=pl.DeviceIdType.MESH)
    for k in range(1, n_quad):
        pl.semaphore_signal(barrier, inc=1, device_id=quad_peer(k)[1], device_id_type=pl.DeviceIdType.MESH)

    for k in range(n_dp * SUB):
        tstage[k : k + 1, :] = tok_ref[0:1, k * lanes : (k + 1) * lanes].astype(jnp.float32)
    for h in range(n_dp):
        tsend[h] = tstage[h * SUB : (h + 1) * SUB, :].astype(jnp.bfloat16)
    pl.semaphore_wait(barrier, n_line - 1 + n_quad - 1)

    sends = []
    for k in range(1, n_line):
        peer, where = line_peer(k)
        copy = remote(tsend.at[to_d[k % n_dp]], tline.at[line], ts_send.at[k], ts_recv.at[k], where)
        copy.start()
        sends.append(copy)
    tline[line] = tsend[d]
    for k in range(1, n_line):
        source = line_source(k)
        remote(tsend.at[0], tline.at[source], ts_send.at[k], ts_recv.at[k], sibling).wait_recv()

    for k in range(1, n_quad):
        copy = remote(tline, tall.at[quad], tq_send.at[k], tq_recv.at[k], quad_peer(k)[1])
        copy.start()
        sends.append(copy)
    tall[quad] = tline[...]
    for k in range(1, n_quad):
        source = quad_source(k)
        remote(tline, tall.at[source], tq_send.at[k], tq_recv.at[k], sibling).wait_recv()
    pair = 2 * n_line
    for p in range(n_quad // 2):
        for i in range(2):
            for s in range(n_line):
                row = (i * n_line + s) * SUB
                block = tall[2 * p + i, s].astype(jnp.float32)
                for b in range(lanes // 128):
                    tflat[b, row : row + SUB, :] = block[:, b * 128 : (b + 1) * 128]
        for s in range(SUB):
            for b in range(lanes // 128):
                part = tflat[b, pl.ds(s, pair, stride=SUB), :]
                col = s * lanes + b * 128
                x[p * pair : (p + 1) * pair, col : col + 128] = part.astype(jnp.bfloat16)

    def finish(j):
        remote(psend.at[j], precv.at[j], p_send.at[j], p_recv.at[j], sibling).wait_recv()
        gate = pown[j, 0] + precv[j, 0].astype(jnp.float32)
        up = pown[j, 1] + precv[j, 1].astype(jnp.float32)
        hid[:, j * cf : (j + 1) * cf] = (gate / (1.0 + jnp.exp(-gate)) * up).astype(jnp.bfloat16)

    for j in range(nf):
        for i, w in enumerate((wg, wu)):
            loads[2 * j + i].wait()
            part = jnp.dot(x[...], w[j], preferred_element_type=jnp.float32)
            pown[j, i] = part
            psend[j, i] = part.astype(jnp.bfloat16)
        copy = remote(psend.at[j], precv.at[j], p_send.at[j], p_recv.at[j], sibling)
        copy.start()
        sends.append(copy)
        if j > 0:
            finish(j - 1)
    finish(nf - 1)

    for j in range(nd):
        loads[2 * nf + j].wait()
        part = jnp.dot(hid[...], wd[j], preferred_element_type=jnp.float32)
        for q in range(n_quad):
            block = part[q * n_line : (q + 1) * n_line]
            osend[j, q] = jnp.concatenate(
                [block[:, i * lanes : (i + 1) * lanes] for i in range(pieces)], axis=0
            ).astype(jnp.bfloat16)
        for k in range(1, n_quad):
            peer, where = quad_peer(k)
            copy = remote(osend.at[j, peer], orecv.at[j, quad], o_send.at[j, k], o_recv.at[j, k], where)
            copy.start()
            sends.append(copy)

    for j in range(nd):
        total = osend[j, quad].astype(jnp.float32)
        for k in range(1, n_quad):
            source = quad_source(k)
            remote(osend.at[j, 0], orecv.at[j, source], o_send.at[j, k], o_recv.at[j, k], sibling).wait_recv()
            total += orecv[j, source].astype(jnp.float32)
        for i in range(pieces):
            for b in range(lanes // 128):
                part = total[i * n_line : (i + 1) * n_line, b * 128 : (b + 1) * 128]
                zstage[b, pl.ds(pieces * j + i, n_line, stride=SUB), :] = part
    for s in range(n_line):
        for b in range(lanes // 128):
            part = zstage[b, s * SUB : (s + 1) * SUB, :]
            zsend[s, :, b * 128 : (b + 1) * 128] = part.astype(jnp.bfloat16)
    for k in range(1, n_line):
        peer, where = line_peer(k)
        copy = remote(zsend.at[peer], zrecv.at[line], z_send.at[k], z_recv.at[k], where)
        copy.start()
        sends.append(copy)
    zrecv[line] = zsend[line]
    for k in range(1, n_line):
        source = line_source(k)
        remote(zsend.at[0], zrecv.at[source], z_send.at[k], z_recv.at[k], sibling).wait_recv()

    for h in range(n_dp):
        total = jnp.zeros((SUB, lanes), jnp.float32)
        for i in range(n_expert):
            weight = jnp.float32(0)
            for c in range(routes_ref.shape[1]):
                weight += jnp.where(routes_ref[0, c] == i, gates_ref[0, c], jnp.float32(0))
            total += weight * zrecv[i * n_dp + h].astype(jnp.float32)
        tstage[h * SUB : (h + 1) * SUB, :] = total
    for k in range(n_dp * SUB):
        out_ref[0:1, k * lanes : (k + 1) * lanes] = tstage[k : k + 1, :].astype(jnp.bfloat16)
    for copy in sends:
        copy.wait_send()


def shards(sizes, tokens, routes, gates, w_gate, w_up, w_down):
    n_groups, n_tensor, n_expert, n_dp = sizes
    n_quad, n_line = n_groups * n_tensor, n_expert * n_dp
    rows = n_quad * n_line
    depth, ffh = w_gate.shape[1], w_gate.shape[2] // n_groups
    cf = min(1024, ffh)
    nf = ffh // cf
    lanes = depth // SUB
    cd = 4 * lanes
    nd = depth // cd
    bf16, f32 = jnp.bfloat16, jnp.float32
    dma = pltpu.SemaphoreType.DMA
    return pl.pallas_call(
        functools.partial(kernel, sizes),
        out_shape=jax.ShapeDtypeStruct(tokens.shape, bf16),
        in_specs=[
            pl.BlockSpec(memory_space=pltpu.VMEM),
            pl.BlockSpec(memory_space=pltpu.SMEM),
            pl.BlockSpec(memory_space=pltpu.SMEM),
            pl.BlockSpec(memory_space=pl.ANY),
            pl.BlockSpec(memory_space=pl.ANY),
            pl.BlockSpec(memory_space=pl.ANY),
        ],
        out_specs=pl.BlockSpec(memory_space=pltpu.VMEM),
        scratch_shapes=[
            pltpu.VMEM((nf, depth, cf), bf16),
            pltpu.VMEM((nf, depth, cf), bf16),
            pltpu.VMEM((nd, ffh, cd), bf16),
            pltpu.VMEM((n_dp * SUB, lanes), f32),
            pltpu.VMEM((n_dp, SUB, lanes), bf16),
            pltpu.VMEM((n_line, SUB, lanes), bf16),
            pltpu.VMEM((n_quad, n_line, SUB, lanes), bf16),
            pltpu.VMEM((lanes // 128, 2 * n_line * SUB, 128), f32),
            pltpu.VMEM((rows, depth), bf16),
            pltpu.VMEM((nf, 2, rows, cf), f32),
            pltpu.VMEM((nf, 2, rows, cf), bf16),
            pltpu.VMEM((nf, 2, rows, cf), bf16),
            pltpu.VMEM((rows, ffh), bf16),
            pltpu.VMEM((nd, n_quad, cd // lanes * n_line, lanes), bf16),
            pltpu.VMEM((nd, n_quad, cd // lanes * n_line, lanes), bf16),
            pltpu.VMEM((lanes // 128, n_line * SUB, 128), f32),
            pltpu.VMEM((n_line, SUB, lanes), bf16),
            pltpu.VMEM((n_line, SUB, lanes), bf16),
            dma((3, max(nf, nd))),
            dma((n_line,)),
            dma((n_line,)),
            dma((n_quad,)),
            dma((n_quad,)),
            dma((nf,)),
            dma((nf,)),
            dma((nd, n_quad)),
            dma((nd, n_quad)),
            dma((n_line,)),
            dma((n_line,)),
        ],
        compiler_params=pltpu.CompilerParams(
            collective_id=0, has_side_effects=True, vmem_limit_bytes=56 * 1024 * 1024
        ),
    )(tokens, routes, gates, w_gate, w_up, w_down)


def solution(mesh):
    placed = (
        P(AXES, None),
        P(AXES, None),
        P(AXES, None),
        P("expert", "dp", "tensor"),
        P("expert", "dp", "tensor"),
        P("expert", "tensor", "dp"),
    )
    return jax.shard_map(
        functools.partial(shards, tuple(mesh.shape[axis] for axis in AXES)),
        mesh=mesh,
        in_specs=placed,
        out_specs=P(AXES, None),
        check_vma=False,
    )
```
